32 devices in a mesh: row: 8 (over z, y), col: 4 (over x, core).
Axes of the slice: x: 2, y: 2, z: 4, core: 2. Of those that a mesh axis runs over, the one named last changes fastest.
Arguments:
- activations: float32 [512, 12288], P('col', 'row'), may hold values from -1.5 to 1.5
- weights: float32 [12288, 24576], P('row', 'col'), may hold values from -0.21875 to 0.21875
- upstream: float32 [512, 24576], P('row', 'col'), may hold values from -6 to 6
Outputs:
- input_grad: float32 [512, 12288], P('col', 'row')
- weight_grad: float32 [12288, 24576], P('row', 'col')
The draws below stay inside these ranges and needn't reach their ends.
All inputs are finite; a program needn't handle non-finite values.
Results may differ from the reference program's by a relative error of at most 0.00009.
Values sent between devices are 32-bit elements; how exact they have to be, the bound alone decides.
A program may use at most 192 MiB of HBM per device.

```python
import jax
import jax.numpy as jnp
from jax import lax

D = 12288
FF = 24576
TOKENS = 512


def levels(stream_key, shape, shards, smallest, largest):
    def one(dim, blocks):
        draws = jax.random.uniform(jax.random.fold_in(jax.random.fold_in(stream_key, 6), dim), (blocks,), jnp.float32, smallest / len(shards), largest / len(shards))
        return jnp.repeat(jnp.exp(draws), shape[dim] // blocks).reshape((-1,) + (1,) * (len(shape) - dim - 1))

    level = one(*shards[0])
    for cut in shards[1:]:
        level = level * one(*cut)
    return level


def scatter_about(rng, shape, scale, reach, cuts=(), kind=jnp.bfloat16):
    array = scale * jax.random.normal(rng, shape, jnp.float32)
    if cuts:
        array = array * levels(rng, shape, cuts, -0.22, 0.18)
    return jnp.clip(array, -reach, reach).astype(kind)


def setup_inputs(seed: int = 0) -> dict:
    splits = jax.random.split(jax.random.key(seed), 4)
    return {
        "activations": scatter_about(splits[0], (TOKENS, D), 0.25, 1.5, ((0, 4), (1, 8)), jnp.float32),
        "weights": scatter_about(splits[1], (D, FF), (D // 16) ** -0.5, 0.21875, ((0, 8), (1, 4)), jnp.float32),
        "upstream": scatter_about(splits[2], (TOKENS, FF), 1.0, 6.0, ((0, 8), (1, 4)), jnp.float32),
    }


slope_scale = 0.7978845608028654
cubic_term = 0.044715


def gelu_slope(preact):
    inner = slope_scale * (preact + cubic_term * preact * preact * preact)
    tangent = jnp.tanh(inner)
    return 0.5 * (1.0 + tangent) + 0.5 * preact * (1.0 - tangent * tangent) * slope_scale * (1.0 + 3.0 * cubic_term * preact * preact)


def reference(activations, weights, upstream):
    preact = jnp.dot(activations, weights, precision=lax.Precision.HIGHEST, preferred_element_type=jnp.float32)
    delta_pre = upstream * gelu_slope(preact)
    input_grad = lax.dot_general(delta_pre, weights, (((1,), (1,)), ((), ())), precision=lax.Precision.HIGHEST, preferred_element_type=jnp.float32)
    weight_grad = lax.dot_general(activations, delta_pre, (((0,), (0,)), ((), ())), precision=lax.Precision.HIGHEST, preferred_element_type=jnp.float32)
    return input_grad, weight_grad
```

```python
import functools

import jax
import jax.numpy as jnp
from jax import lax
from jax.experimental import pallas as pl
from jax.experimental.pallas import tpu as pltpu
from jax.sharding import PartitionSpec as P

slope_scale = 0.7978845608028654
cubic_term = 0.044715
MESH = pl.DeviceIdType.MESH
LANES = 128
OUTER = 4


def gelu_slope(preact):
    inner = slope_scale * (preact + cubic_term * preact * preact * preact)
    tangent = jnp.tanh(inner)
    return 0.5 * (1.0 + tangent) + 0.5 * preact * (1.0 - tangent * tangent) * slope_scale * (
        1.0 + 3.0 * cubic_term * preact * preact
    )


def split(value):
    high = value.astype(jnp.bfloat16)
    return high, (value - high.astype(jnp.float32)).astype(jnp.bfloat16)


def dot3(a_high, a_low, b_high, b_low, dims):
    def one(a, b):
        return lax.dot_general(a, b, (dims, ((), ())), preferred_element_type=jnp.float32)

    return one(a_high, b_high) + (one(a_high, b_low) + one(a_low, b_high))


class Stream:
    def __init__(self, first, second, refs, tokens):
        self.axes = (first, second)
        self.state, self.land_first, self.land_second, self.send, self.recv, self.ready = refs
        (n_f, _, _), (n_g, _, _) = first, second
        self.big, self.small = tokens // n_f, tokens // (n_f * n_g)
        self.hops = (
            [("sum", 0, h) for h in range(1, n_f)]
            + [("sum", 1, h) for h in range(1, n_g)]
            + [("spread", 1, h) for h in range(1, n_g)]
            + [("spread", 0, h) for h in range(1, n_f)]
        )
        self.sums = n_f + n_g - 2

    def region(self, axis, block):
        if axis == 0:
            return pl.ds(pl.multiple_of(block * self.big, self.big), self.big)
        mine = self.axes[0][1] * self.big
        return pl.ds(pl.multiple_of(mine + block * self.small, self.small), self.small)

    def own(self):
        return self.region(1, self.axes[1][1])

    def copy(self, j, way, slot, block, row, col):
        kind, axis, h = self.hops[j]
        n, me, stride = self.axes[axis]
        peer = row + stride if way == 0 else row - stride
        source = self.state.at[slot, self.region(axis, block)]
        if kind == "sum":
            land = self.land_first if axis == 0 else self.land_second
            target = land.at[h - 1, way]
        else:
            target = source
        return pltpu.make_async_remote_copy(
            src_ref=source,
            dst_ref=target,
            send_sem=self.send.at[j, way],
            recv_sem=self.recv.at[j, way],
            device_id=(peer, col),
            device_id_type=MESH,
        )

    def sending(self, j, way):
        kind, axis, h = self.hops[j]
        n, me, _ = self.axes[axis]
        if kind == "sum":
            if way == 0:
                return jnp.logical_and(me <= h - 1, me < n - 1), n - h + me
            return jnp.logical_and(n - 1 - me <= h - 1, me > 0), h - n + me
        if way == 0:
            return jnp.logical_and(me >= h - 1, me < n - 1), me - (h - 1)
        return jnp.logical_and(n - 1 - me >= h - 1, me > 0), me + (h - 1)

    def receiving(self, j, way):
        kind, axis, h = self.hops[j]
        n, me, _ = self.axes[axis]
        if kind == "sum":
            if way == 0:
                return jnp.logical_and(me <= h, me >= 1), n - h + me - 1
            return jnp.logical_and(n - 1 - me <= h, me <= n - 2), h - n + me + 1
        if way == 0:
            return me >= h, me - h
        return n - 1 - me >= h, me + h

    def issue(self, step, chunks, slots, row, col):
        for j in range(len(self.hops)):
            chunk = step - 1 - j
            valid = jnp.logical_and(chunk >= 0, chunk < chunks)
            slot = lax.rem(chunk + slots, slots)
            for way in range(2):
                on, block = self.sending(j, way)

                @pl.when(jnp.logical_and(valid, on))
                def _(j=j, way=way, slot=slot, block=block):
                    self.copy(j, way, slot, block, row, col).start()

    def settle(self, step, chunks, slots, row, col, finish):
        for j in range(len(self.hops)):
            chunk = step - 2 - j
            valid = jnp.logical_and(chunk >= 0, chunk < chunks)
            slot = lax.rem(chunk + 2 * slots, slots)
            kind, axis, h = self.hops[j]
            for way in range(2):
                sent, out_block = self.sending(j, way)

                @pl.when(jnp.logical_and(valid, sent))
                def _(j=j, way=way, slot=slot, block=out_block):
                    self.copy(j, way, slot, block, row, col).wait_send()

                got, in_block = self.receiving(j, way)

                @pl.when(jnp.logical_and(valid, got))
                def _(j=j, way=way, slot=slot, block=in_block, kind=kind, axis=axis, h=h):
                    self.copy(j, way, slot, block, row, col).wait_recv()
                    if kind == "sum":
                        land = self.land_first if axis == 0 else self.land_second
                        here = self.region(axis, block)
                        self.state[slot, here, :] = self.state[slot, here, :] + land[h - 1, way]

            if j == self.sums - 1:

                @pl.when(valid)
                def _(slot=slot, chunk=chunk):
                    finish(slot, chunk)


def exchange_kernel(
    outer,
    inner,
    act_ref,
    up_ref,
    w_ref,
    high_ref,
    low_ref,
    grad_ref,
    w_in,
    w_high,
    w_low,
    g_high,
    g_low,
    state_a,
    state_b,
    land_a1,
    land_a2,
    land_b1,
    land_b2,
    send_a,
    recv_a,
    send_b,
    recv_b,
    ready_a,
    ready_b,
    w_sem,
):
    tokens, depth = act_ref.shape
    columns = up_ref.shape[1]
    width = 2 * LANES
    chunks = columns // width
    slots = state_a.shape[0]
    part = tokens // (outer * inner)
    tile = min(256, tokens)
    row, col = lax.axis_index("row"), lax.axis_index("col")
    at_outer, at_inner = row // inner, lax.rem(row, inner)
    along_outer = (outer, at_outer, inner)
    along_inner = (inner, at_inner, 1)
    stream_a = Stream(along_inner, along_outer, (state_a, land_a1, land_a2, send_a, recv_a, ready_a), tokens)
    stream_b = Stream(along_outer, along_inner, (state_b, land_b1, land_b2, send_b, recv_b, ready_b), tokens)

    neighbours = []
    for index, (n, me, stride) in enumerate((along_inner, along_outer)):
        neighbours.append((me < n - 1, row + stride, 2 * index, 2 * index + 1))
        neighbours.append((me > 0, row - stride, 2 * index + 1, 2 * index))

    barrier = pltpu.get_barrier_semaphore()
    for there, peer, _, _ in neighbours:

        @pl.when(there)
        def _(peer=peer):
            pl.semaphore_signal(barrier, inc=1, device_id=(peer, col), device_id_type=MESH)

    pl.semaphore_wait(barrier, sum(there.astype(jnp.int32) for there, _, _, _ in neighbours))

    def meet(ready):
        for there, peer, _, theirs in neighbours:

            @pl.when(there)
            def _(peer=peer, theirs=theirs):
                pl.semaphore_signal(ready.at[theirs], inc=1, device_id=(peer, col), device_id_type=MESH)

        for there, _, mine, _ in neighbours:

            @pl.when(there)
            def _(mine=mine):
                pl.semaphore_wait(ready.at[mine], 1)

    def load(chunk):
        at = pl.ds(pl.multiple_of(chunk * width, width), width)
        here = lax.rem(chunk, 2)
        return pltpu.make_async_copy(w_ref.at[:, at], w_in.at[here], w_sem.at[here])

    load(0).start()

    @pl.loop(0, tokens // tile)
    def _(i):
        at = pl.ds(pl.multiple_of(i * tile, tile), tile)
        g_high[at, :], g_low[at, :] = split(act_ref[at, :])

    grad_ref[...] = jnp.zeros_like(grad_ref)

    def finish(stream, half):
        def run(slot, chunk):
            own = stream.own()
            at = pl.ds(pl.multiple_of(chunk * width + half * LANES, LANES), LANES)
            stream.state[slot, own, :] = up_ref[:, at] * gelu_slope(stream.state[slot, own, :])

        return run

    def swapped(index):
        place = lax.rem(index, inner) * outer + index // inner
        return pl.ds(pl.multiple_of(place * part, part), part)

    w_tile = 128

    def forward(chunk):
        slot = lax.rem(chunk, slots)
        here = lax.rem(chunk, 2)

        @pl.loop(0, depth // w_tile)
        def _(i):
            at = pl.ds(pl.multiple_of(i * w_tile, w_tile), w_tile)
            w_high[slot, at, :], w_low[slot, at, :] = split(w_in[here, at, :])

        @pl.loop(0, tokens // tile)
        def _(i):
            at = pl.ds(pl.multiple_of(i * tile, tile), tile)
            product = dot3(
                g_high[at, :], g_low[at, :], w_high[slot], w_low[slot], ((1,), (0,))
            )
            state_b[slot, at, :] = product[:, LANES:]
            for q in range(tile // part):
                state_a[slot, swapped(i * (tile // part) + q), :] = product[
                    q * part : (q + 1) * part, :LANES
                ]

    def backward(chunk):
        slot = lax.rem(chunk, slots)
        left = pl.ds(pl.multiple_of(chunk * width, width), LANES)
        right = pl.ds(pl.multiple_of(chunk * width + LANES, LANES), LANES)
        both = pl.ds(pl.multiple_of(chunk * width, width), width)

        @pl.loop(0, tokens // part)
        def _(i):
            at = pl.ds(pl.multiple_of(i * part, part), part)
            high_ref[at, left], low_ref[at, left] = split(state_a[slot, swapped(i), :])
            high_ref[at, right], low_ref[at, right] = split(state_b[slot, at, :])

        @pl.loop(0, tokens // tile)
        def _(i):
            at = pl.ds(pl.multiple_of(i * tile, tile), tile)
            grad_ref[at, :] += dot3(
                high_ref[at, both], low_ref[at, both], w_high[slot], w_low[slot], ((1,), (1,))
            )

    hops = len(stream_a.hops)

    @pl.loop(0, chunks + hops + 1)
    def _(step):
        stream_a.settle(step, chunks, slots, row, col, finish(stream_a, 0))
        meet(ready_a)
        stream_a.issue(step, chunks, slots, row, col)

        @pl.when(step < chunks)
        def _():
            load(step).wait()

            @pl.when(step + 1 < chunks)
            def _():
                load(step + 1).start()

            forward(step)

        stream_b.settle(step, chunks, slots, row, col, finish(stream_b, 1))
        meet(ready_b)
        stream_b.issue(step, chunks, slots, row, col)

        @pl.when(step >= hops + 1)
        def _():
            backward(step - (hops + 1))


def exchange(activations, upstream, weights, outer, inner):
    tokens, depth = activations.shape
    columns = weights.shape[1]
    width = 2 * LANES
    hops = 2 * (outer + inner - 2)
    slots = hops + 2
    f32, bf16 = jnp.float32, jnp.bfloat16
    small = tokens // (outer * inner)
    whole = pl.BlockSpec(memory_space=pltpu.VMEM)
    return pl.pallas_call(
        functools.partial(exchange_kernel, outer, inner),
        out_shape=(
            jax.ShapeDtypeStruct((tokens, columns), bf16),
            jax.ShapeDtypeStruct((tokens, columns), bf16),
            jax.ShapeDtypeStruct((tokens, depth), f32),
        ),
        in_specs=[whole, whole, pl.BlockSpec(memory_space=pl.ANY)],
        out_specs=(whole, whole, whole),
        scratch_shapes=[
            pltpu.VMEM((2, depth, width), f32),
            pltpu.VMEM((slots, depth, width), bf16),
            pltpu.VMEM((slots, depth, width), bf16),
            pltpu.VMEM((tokens, depth), bf16),
            pltpu.VMEM((tokens, depth), bf16),
            pltpu.VMEM((slots, tokens, LANES), f32),
            pltpu.VMEM((slots, tokens, LANES), f32),
            pltpu.VMEM((inner - 1, 2, tokens // inner, LANES), f32),
            pltpu.VMEM((outer - 1, 2, small, LANES), f32),
            pltpu.VMEM((outer - 1, 2, tokens // outer, LANES), f32),
            pltpu.VMEM((inner - 1, 2, small, LANES), f32),
            pltpu.SemaphoreType.DMA((hops, 2)),
            pltpu.SemaphoreType.DMA((hops, 2)),
            pltpu.SemaphoreType.DMA((hops, 2)),
            pltpu.SemaphoreType.DMA((hops, 2)),
            pltpu.SemaphoreType.REGULAR((4,)),
            pltpu.SemaphoreType.REGULAR((4,)),
            pltpu.SemaphoreType.DMA((2,)),
        ],
        compiler_params=pltpu.CompilerParams(
            collective_id=0, has_side_effects=True, vmem_limit_bytes=58 * 1024 * 1024
        ),
        cost_estimate=pl.CostEstimate(
            flops=12 * tokens * depth * columns,
            bytes_accessed=4 * depth * columns,
            transcendentals=small * columns,
        ),
    )(activations, upstream, weights)


def outer_product_kernel(act_ref, high_ref, low_ref, out_ref, a_high, a_low):
    @pl.when(pl.program_id(0) == 0)
    def _():
        a_high[...], a_low[...] = split(act_ref[...])

    tile = 256 if out_ref.shape[0] % 256 == 0 else 128

    @pl.loop(0, out_ref.shape[0] // tile)
    def _(i):
        at = pl.ds(pl.multiple_of(i * tile, tile), tile)
        out_ref[at, :] = dot3(
            a_high[at, :], a_low[at, :], high_ref[...], low_ref[...], ((1,), (0,))
        )


def outer_product(features, high, low):
    depth, tokens = features.shape
    columns = high.shape[1]
    width = 512
    return pl.pallas_call(
        outer_product_kernel,
        out_shape=jax.ShapeDtypeStruct((depth, columns), jnp.float32),
        grid=(columns // width,),
        in_specs=[
            pl.BlockSpec((depth, tokens), lambda i: (0, 0)),
            pl.BlockSpec((tokens, width), lambda i: (0, i)),
            pl.BlockSpec((tokens, width), lambda i: (0, i)),
        ],
        out_specs=pl.BlockSpec((depth, width), lambda i: (0, i)),
        scratch_shapes=[
            pltpu.VMEM((depth, tokens), jnp.bfloat16),
            pltpu.VMEM((depth, tokens), jnp.bfloat16),
        ],
        compiler_params=pltpu.CompilerParams(vmem_limit_bytes=40 * 1024 * 1024),
        cost_estimate=pl.CostEstimate(
            flops=6 * tokens * depth * columns,
            bytes_accessed=4 * depth * columns + 4 * tokens * columns,
            transcendentals=0,
        ),
    )(features, high, low)


def body(rows, activations, weights, upstream):
    gathered = lax.all_gather(activations, "col", axis=0, tiled=True)
    high, low, grad = exchange(gathered, upstream, weights, OUTER, rows // OUTER)
    input_grad = lax.psum_scatter(grad, "col", scatter_dimension=0, tiled=True)
    weight_grad = outer_product(gathered.T, high, low)
    return (input_grad, weight_grad)


def solution(mesh):
    placed = (P("col", "row"), P("row", "col"), P("row", "col"))
    return jax.shard_map(
        functools.partial(body, mesh.shape["row"]),
        mesh=mesh,
        in_specs=placed,
        out_specs=(P("col", "row"), P("row", "col")),
        check_vma=False,
    )
```

```python
import functools

import jax
import jax.numpy as jnp
from jax import lax
from jax.experimental import pallas as pl
from jax.experimental.pallas import tpu as pltpu
from jax.sharding import PartitionSpec as P

slope_scale = 0.7978845608028654
cubic_term = 0.044715
MESH = pl.DeviceIdType.MESH
LANES = 128
OUTER = 4


def gelu_slope(preact):
    inner = slope_scale * (preact + cubic_term * preact * preact * preact)
    tangent = jnp.tanh(inner)
    return 0.5 * (1.0 + tangent) + 0.5 * preact * (1.0 - tangent * tangent) * slope_scale * (
        1.0 + 3.0 * cubic_term * preact * preact
    )


def split(value):
    high = value.astype(jnp.bfloat16)
    return high, (value - high.astype(jnp.float32)).astype(jnp.bfloat16)


def dot3(a_high, a_low, b_high, b_low, dims):
    def one(a, b):
        return lax.dot_general(a, b, (dims, ((), ())), preferred_element_type=jnp.float32)

    return one(a_high, b_high) + (one(a_high, b_low) + one(a_low, b_high))


class Stream:
    def __init__(self, first, second, refs, tokens):
        self.axes = (first, second)
        self.state, self.land_first, self.land_second, self.send, self.recv, self.ready = refs
        (n_f, _, _), (n_g, _, _) = first, second
        self.big, self.small = tokens // n_f, tokens // (n_f * n_g)
        self.hops = (
            [("sum", 0, h) for h in range(1, n_f)]
            + [("sum", 1, h) for h in range(1, n_g)]
            + [("spread", 1, h) for h in range(1, n_g)]
            + [("spread", 0, h) for h in range(1, n_f)]
        )
        self.sums = n_f + n_g - 2

    def region(self, axis, block):
        if axis == 0:
            return pl.ds(pl.multiple_of(block * self.big, self.big), self.big)
        mine = self.axes[0][1] * self.big
        return pl.ds(pl.multiple_of(mine + block * self.small, self.small), self.small)

    def own(self):
        return self.region(1, self.axes[1][1])

    def copy(self, j, way, slot, block, row, col):
        kind, axis, h = self.hops[j]
        n, me, stride = self.axes[axis]
        peer = row + stride if way == 0 else row - stride
        source = self.state.at[slot, self.region(axis, block)]
        if kind == "sum":
            land = self.land_first if axis == 0 else self.land_second
            target = land.at[h - 1, way]
        else:
            target = source
        return pltpu.make_async_remote_copy(
            src_ref=source,
            dst_ref=target,
            send_sem=self.send.at[j, way],
            recv_sem=self.recv.at[j, way],
            device_id=(peer, col),
            device_id_type=MESH,
        )

    def sending(self, j, way):
        kind, axis, h = self.hops[j]
        n, me, _ = self.axes[axis]
        if kind == "sum":
            if way == 0:
                return jnp.logical_and(me <= h - 1, me < n - 1), n - h + me
            return jnp.logical_and(n - 1 - me <= h - 1, me > 0), h - n + me
        if way == 0:
            return jnp.logical_and(me >= h - 1, me < n - 1), me - (h - 1)
        return jnp.logical_and(n - 1 - me >= h - 1, me > 0), me + (h - 1)

    def receiving(self, j, way):
        kind, axis, h = self.hops[j]
        n, me, _ = self.axes[axis]
        if kind == "sum":
            if way == 0:
                return jnp.logical_and(me <= h, me >= 1), n - h + me - 1
            return jnp.logical_and(n - 1 - me <= h, me <= n - 2), h - n + me + 1
        if way == 0:
            return me >= h, me - h
        return n - 1 - me >= h, me + h

    def issue(self, step, chunks, slots, row, col):
        for j in range(len(self.hops)):
            chunk = step - 1 - j
            valid = jnp.logical_and(chunk >= 0, chunk < chunks)
            slot = lax.rem(chunk + slots, slots)
            for way in range(2):
                on, block = self.sending(j, way)

                @pl.when(jnp.logical_and(valid, on))
                def _(j=j, way=way, slot=slot, block=block):
                    self.copy(j, way, slot, block, row, col).start()

    def settle(self, step, chunks, slots, row, col, finish):
        for j in range(len(self.hops)):
            chunk = step - 2 - j
            valid = jnp.logical_and(chunk >= 0, chunk < chunks)
            slot = lax.rem(chunk + 2 * slots, slots)
            kind, axis, h = self.hops[j]
            for way in range(2):
                sent, out_block = self.sending(j, way)

                @pl.when(jnp.logical_and(valid, sent))
                def _(j=j, way=way, slot=slot, block=out_block):
                    self.copy(j, way, slot, block, row, col).wait_send()

                got, in_block = self.receiving(j, way)

                @pl.when(jnp.logical_and(valid, got))
                def _(j=j, way=way, slot=slot, block=in_block, kind=kind, axis=axis, h=h):
                    self.copy(j, way, slot, block, row, col).wait_recv()
                    if kind == "sum":
                        land = self.land_first if axis == 0 else self.land_second
                        here = self.region(axis, block)
                        self.state[slot, here, :] = self.state[slot, here, :] + land[h - 1, way]

            if j == self.sums - 1:

                @pl.when(valid)
                def _(slot=slot, chunk=chunk):
                    finish(slot, chunk)


def exchange_kernel(
    outer,
    inner,
    act_ref,
    up_ref,
    w_ref,
    high_ref,
    low_ref,
    grad_ref,
    w_in,
    w_high,
    w_low,
    g_high,
    g_low,
    state_a,
    state_b,
    land_a1,
    land_a2,
    land_b1,
    land_b2,
    send_a,
    recv_a,
    send_b,
    recv_b,
    ready_a,
    ready_b,
    w_sem,
):
    tokens, depth = act_ref.shape
    columns = up_ref.shape[1]
    width = 2 * LANES
    chunks = columns // width
    slots = state_a.shape[0]
    part = tokens // (outer * inner)
    tile = min(256, tokens)
    row, col = lax.axis_index("row"), lax.axis_index("col")
    at_outer, at_inner = row // inner, lax.rem(row, inner)
    along_outer = (outer, at_outer, inner)
    along_inner = (inner, at_inner, 1)
    stream_a = Stream(along_inner, along_outer, (state_a, land_a1, land_a2, send_a, recv_a, ready_a), tokens)
    stream_b = Stream(along_outer, along_inner, (state_b, land_b1, land_b2, send_b, recv_b, ready_b), tokens)

    neighbours = []
    for index, (n, me, stride) in enumerate((along_inner, along_outer)):
        neighbours.append((me < n - 1, row + stride, 2 * index, 2 * index + 1))
        neighbours.append((me > 0, row - stride, 2 * index + 1, 2 * index))

    barrier = pltpu.get_barrier_semaphore()
    for there, peer, _, _ in neighbours:

        @pl.when(there)
        def _(peer=peer):
            pl.semaphore_signal(barrier, inc=1, device_id=(peer, col), device_id_type=MESH)

    pl.semaphore_wait(barrier, sum(there.astype(jnp.int32) for there, _, _, _ in neighbours))

    def meet(ready):
        for there, peer, _, theirs in neighbours:

            @pl.when(there)
            def _(peer=peer, theirs=theirs):
                pl.semaphore_signal(ready.at[theirs], inc=1, device_id=(peer, col), device_id_type=MESH)

        for there, _, mine, _ in neighbours:

            @pl.when(there)
            def _(mine=mine):
                pl.semaphore_wait(ready.at[mine], 1)

    def load(chunk):
        at = pl.ds(pl.multiple_of(chunk * width, width), width)
        here = lax.rem(chunk, 2)
        return pltpu.make_async_copy(w_ref.at[:, at], w_in.at[here], w_sem.at[here])

    load(0).start()

    @pl.loop(0, tokens // tile)
    def _(i):
        at = pl.ds(pl.multiple_of(i * tile, tile), tile)
        g_high[at, :], g_low[at, :] = split(act_ref[at, :])

    grad_ref[...] = jnp.zeros_like(grad_ref)

    def finish(stream, half):
        def run(slot, chunk):
            own = stream.own()
            at = pl.ds(pl.multiple_of(chunk * width + half * LANES, LANES), LANES)
            stream.state[slot, own, :] = up_ref[:, at] * gelu_slope(stream.state[slot, own, :])

        return run

    def swapped(index):
        place = lax.rem(index, inner) * outer + index // inner
        return pl.ds(pl.multiple_of(place * part, part), part)

    w_tile = 128

    def forward(chunk):
        slot = lax.rem(chunk, slots)
        here = lax.rem(chunk, 2)

        @pl.loop(0, depth // w_tile)
        def _(i):
            at = pl.ds(pl.multiple_of(i * w_tile, w_tile), w_tile)
            w_high[slot, at, :], w_low[slot, at, :] = split(w_in[here, at, :])

        @pl.loop(0, tokens // tile)
        def _(i):
            at = pl.ds(pl.multiple_of(i * tile, tile), tile)
            product = dot3(
                g_high[at, :], g_low[at, :], w_high[slot], w_low[slot], ((1,), (0,))
            )
            state_b[slot, at, :] = product[:, LANES:]
            for q in range(tile // part):
                state_a[slot, swapped(i * (tile // part) + q), :] = product[
                    q * part : (q + 1) * part, :LANES
                ]

    def backward(chunk):
        slot = lax.rem(chunk, slots)
        left = pl.ds(pl.multiple_of(chunk * width, width), LANES)
        right = pl.ds(pl.multiple_of(chunk * width + LANES, LANES), LANES)
        both = pl.ds(pl.multiple_of(chunk * width, width), width)

        @pl.loop(0, tokens // part)
        def _(i):
            at = pl.ds(pl.multiple_of(i * part, part), part)
            high_ref[at, left], low_ref[at, left] = split(state_a[slot, swapped(i), :])
            high_ref[at, right], low_ref[at, right] = split(state_b[slot, at, :])

        @pl.loop(0, tokens // tile)
        def _(i):
            at = pl.ds(pl.multiple_of(i * tile, tile), tile)
            grad_ref[at, :] += dot3(
                high_ref[at, both], low_ref[at, both], w_high[slot], w_low[slot], ((1,), (1,))
            )

    hops = len(stream_a.hops)

    @pl.loop(0, chunks + hops + 1)
    def _(step):
        stream_a.settle(step, chunks, slots, row, col, finish(stream_a, 0))
        meet(ready_a)
        stream_a.issue(step, chunks, slots, row, col)

        @pl.when(step < chunks)
        def _():
            load(step).wait()

            @pl.when(step + 1 < chunks)
            def _():
                load(step + 1).start()

            forward(step)

        stream_b.settle(step, chunks, slots, row, col, finish(stream_b, 1))
        meet(ready_b)
        stream_b.issue(step, chunks, slots, row, col)

        @pl.when(step >= hops + 1)
        def _():
            backward(step - (hops + 1))


def exchange(activations, upstream, weights, outer, inner):
    tokens, depth = activations.shape
    columns = weights.shape[1]
    width = 2 * LANES
    hops = 2 * (outer + inner - 2)
    slots = hops + 2
    f32, bf16 = jnp.float32, jnp.bfloat16
    small = tokens // (outer * inner)
    whole = pl.BlockSpec(memory_space=pltpu.VMEM)
    return pl.pallas_call(
        functools.partial(exchange_kernel, outer, inner),
        out_shape=(
            jax.ShapeDtypeStruct((tokens, columns), bf16),
            jax.ShapeDtypeStruct((tokens, columns), bf16),
            jax.ShapeDtypeStruct((tokens, depth), f32),
        ),
        in_specs=[whole, whole, pl.BlockSpec(memory_space=pl.ANY)],
        out_specs=(whole, whole, whole),
        scratch_shapes=[
            pltpu.VMEM((2, depth, width), f32),
            pltpu.VMEM((slots, depth, width), bf16),
            pltpu.VMEM((slots, depth, width), bf16),
            pltpu.VMEM((tokens, depth), bf16),
            pltpu.VMEM((tokens, depth), bf16),
            pltpu.VMEM((slots, tokens, LANES), f32),
            pltpu.VMEM((slots, tokens, LANES), f32),
            pltpu.VMEM((inner - 1, 2, tokens // inner, LANES), f32),
            pltpu.VMEM((outer - 1, 2, small, LANES), f32),
            pltpu.VMEM((outer - 1, 2, tokens // outer, LANES), f32),
            pltpu.VMEM((inner - 1, 2, small, LANES), f32),
            pltpu.SemaphoreType.DMA((hops, 2)),
            pltpu.SemaphoreType.DMA((hops, 2)),
            pltpu.SemaphoreType.DMA((hops, 2)),
            pltpu.SemaphoreType.DMA((hops, 2)),
            pltpu.SemaphoreType.REGULAR((4,)),
            pltpu.SemaphoreType.REGULAR((4,)),
            pltpu.SemaphoreType.DMA((2,)),
        ],
        compiler_params=pltpu.CompilerParams(
            collective_id=0, has_side_effects=True, vmem_limit_bytes=58 * 1024 * 1024
        ),
        cost_estimate=pl.CostEstimate(
            flops=12 * tokens * depth * columns,
            bytes_accessed=4 * depth * columns,
            transcendentals=small * columns,
        ),
    )(activations, upstream, weights)


def outer_product_kernel(act_ref, high_ref, low_ref, out_ref, left, right):
    tokens = act_ref.shape[0]

    @pl.when(pl.program_id(0) == 0)
    def _():
        high, low = split(act_ref[...].T)
        left[:, :tokens] = high
        left[:, tokens : 2 * tokens] = high
        left[:, 2 * tokens :] = low

    right[:tokens, :] = high_ref[...]
    right[tokens : 2 * tokens, :] = low_ref[...]
    right[2 * tokens :, :] = high_ref[...]
    tile = 256 if out_ref.shape[0] % 256 == 0 else 128

    @pl.loop(0, out_ref.shape[0] // tile)
    def _(i):
        at = pl.ds(pl.multiple_of(i * tile, tile), tile)
        out_ref[at, :] = jnp.dot(left[at, :], right[...], preferred_element_type=jnp.float32)


def outer_product(features, high, low):
    tokens, depth = features.shape
    columns = high.shape[1]
    width = 512
    return pl.pallas_call(
        outer_product_kernel,
        out_shape=jax.ShapeDtypeStruct((depth, columns), jnp.float32),
        grid=(columns // width,),
        in_specs=[
            pl.BlockSpec((tokens, depth), lambda i: (0, 0)),
            pl.BlockSpec((tokens, width), lambda i: (0, i)),
            pl.BlockSpec((tokens, width), lambda i: (0, i)),
        ],
        out_specs=pl.BlockSpec((depth, width), lambda i: (0, i)),
        scratch_shapes=[
            pltpu.VMEM((depth, 3 * tokens), jnp.bfloat16),
            pltpu.VMEM((3 * tokens, width), jnp.bfloat16),
        ],
        compiler_params=pltpu.CompilerParams(vmem_limit_bytes=40 * 1024 * 1024),
        cost_estimate=pl.CostEstimate(
            flops=6 * tokens * depth * columns,
            bytes_accessed=4 * depth * columns + 4 * tokens * columns,
            transcendentals=0,
        ),
    )(features, high, low)


def body(rows, activations, weights, upstream):
    gathered = lax.all_gather(activations, "col", axis=0, tiled=True)
    high, low, grad = exchange(gathered, upstream, weights, OUTER, rows // OUTER)
    input_grad = lax.psum_scatter(grad, "col", scatter_dimension=0, tiled=True)
    weight_grad = outer_product(gathered, high, low)
    return (input_grad, weight_grad)


def solution(mesh):
    placed = (P("col", "row"), P("row", "col"), P("row", "col"))
    return jax.shard_map(
        functools.partial(body, mesh.shape["row"]),
        mesh=mesh,
        in_specs=placed,
        out_specs=(P("col", "row"), P("row", "col")),
        check_vma=False,
    )
```
